256 devices in a mesh: dp: 32 (over z, y_lo, core), hst: 8 (over y_hi, x).
Axes of the slice: x: 4, y: 4 (y_hi: 2, y_lo: 2; y = y_hi * 2 + y_lo), z: 8, core: 2. Of those that a mesh axis runs over, the one named last changes fastest.
Arguments:
- picture_features: bfloat16 [65536, 1152], P(('dp', 'hst')), may hold values from -6 to 6
- caption_features: bfloat16 [65536, 1152], P(('dp', 'hst')), may hold values from -6 to 6
- matching_caption_slot: int32 [32, 2048], P('dp'), may hold values from 0 to 2047, each once within a row
- score_inverse_heat: float32 [1], replicated, may hold values from 8 to 24
- score_offset: float32 [1], replicated, may hold values from -2 to 0.5
Outputs:
- row_loss: float32 [65536], P(('dp', 'hst'))
- grad_image: bfloat16 [65536, 1152], P(('dp', 'hst'))
- grad_text: bfloat16 [65536, 1152], P(('dp', 'hst'))
The draws below stay inside these ranges and needn't reach their ends.
Inputs may be any that keep to these rules, and one draw needn't show every extreme that they name: Each row of matching_caption_slot holds every number of 0 to 2047 once.
All inputs are finite; a program needn't handle non-finite values.
Results may differ from the reference program's by a relative error of at most 0.0051.
Values may be sent and summed in bfloat16 or wider, within the bound.
No kernel may reach another device: no remote copies, remote signals or barrier semaphores. Data moves between devices by JAX's collectives and lax.ppermute only.
A program may use at most 128 MiB of HBM per device.

```python
import math
import jax
import jax.numpy as jnp
from jax import lax

FEATURE_DIM = 1152
GROUP = 2048
TOKENS = 65536
N_DP = 32


def block_levels(own_key, shape, shards, least, top_value):
    factor_of = 1.0
    for axis_at, blocks in shards:
        heights = jax.random.uniform(jax.random.fold_in(jax.random.fold_in(own_key, 6), axis_at), (blocks,), jnp.float32, least / len(shards), top_value / len(shards))
        factor_of = factor_of * jnp.repeat(jnp.exp(heights), shape[axis_at] // blocks).reshape((-1,) + (1,) * (len(shape) - 1 - axis_at))
    return factor_of


def bell_draw(own_key, extent, scale, reach, split=(), kind=jnp.bfloat16):
    result = jax.random.normal(own_key, extent, jnp.float32) * scale
    if len(split) > 0:
        result = block_levels(own_key, extent, split, -0.22, 0.18) * result
    return jnp.clip(result, min=-reach, max=reach).astype(kind)


def setup_inputs(seed: int = 0) -> dict:
    streams_of = jax.random.split(jax.random.key(seed), 6)
    picture_features = bell_draw(streams_of[0], (TOKENS, FEATURE_DIM), 1.0, 6.0, ((0, 256),))
    caption_features = bell_draw(streams_of[1], (TOKENS, FEATURE_DIM), 1.0, 6.0, ((0, 256),))
    matching_caption_slot = jax.vmap(lambda own: jax.random.permutation(own, GROUP))(jax.random.split(streams_of[2], N_DP)).reshape((N_DP, GROUP)).astype(jnp.int32)
    score_inverse_heat = jnp.clip(jnp.exp(jax.random.uniform(streams_of[3], (1,), jnp.float32, math.log(8.0), math.log(24.0))), 8.0, 24.0)
    score_offset = jnp.clip(jax.random.uniform(streams_of[4], (1,), jnp.float32, -2.0, 0.5), -2.0, 0.5)
    return dict(picture_features=picture_features, caption_features=caption_features, matching_caption_slot=matching_caption_slot, score_inverse_heat=score_inverse_heat, score_offset=score_offset)


def pair_logits(image_rows, text_block, score_scaling_factor, offset):
    product = lax.dot_general(image_rows, text_block, (((1,), (1,)), ((), ())), preferred_element_type=jnp.float32)
    return score_scaling_factor * product + offset


def block_terms(image_rows, text_block, score_scaling_factor, offset, positive):
    logits = pair_logits(image_rows, text_block, score_scaling_factor, offset)
    labels = 2.0 * positive - 1.0
    pair_loss = jnp.sum(jax.nn.log_sigmoid(labels * logits), axis=1)
    coefficient = (score_scaling_factor * (jax.nn.sigmoid(logits) - positive)).astype(jnp.bfloat16)
    image_part = jnp.dot(coefficient, text_block, preferred_element_type=jnp.float32)
    text_part = lax.dot_general(coefficient, image_rows, (((0,), (0,)), ((), ())), preferred_element_type=jnp.float32)
    return pair_loss, image_part, text_part


def reference(picture_features, caption_features, matching_caption_slot, score_inverse_heat, score_offset):
    images = picture_features.reshape(N_DP, GROUP, FEATURE_DIM)
    texts = caption_features.reshape(N_DP, GROUP, FEATURE_DIM)
    score_scaling_factor = score_inverse_heat[0] / FEATURE_DIM
    offset = score_offset[0]
    columns = jnp.arange(GROUP, dtype=jnp.int32)

    def group_terms(group_index):
        image_rows = images[group_index]
        positive = (columns[None, :] == matching_caption_slot[group_index][:, None]).astype(jnp.float32)
        nothing = jnp.zeros_like(positive)
        lower_block = texts[(group_index + N_DP - 1) % N_DP]
        upper_block = texts[(group_index + 1) % N_DP]
        own_loss, own_image, own_text = block_terms(image_rows, texts[group_index], score_scaling_factor, offset, positive)
        low_loss, low_image, low_text = block_terms(image_rows, lower_block, score_scaling_factor, offset, nothing)
        up_loss, up_image, up_text = block_terms(image_rows, upper_block, score_scaling_factor, offset, nothing)
        row_loss = -(own_loss + low_loss + up_loss) / (3 * GROUP)
        grad_image = (own_image + low_image + up_image).astype(jnp.bfloat16)
        return row_loss, grad_image, own_text, low_text, up_text

    indices = jnp.arange(N_DP, dtype=jnp.int32)
    row_loss, grad_image, own_text, low_text, up_text = lax.map(group_terms, indices)
    grad_text = own_text + jnp.roll(low_text, -1, axis=0) + jnp.roll(up_text, 1, axis=0)
    return row_loss.reshape(TOKENS), grad_image.reshape(TOKENS, FEATURE_DIM), grad_text.astype(jnp.bfloat16).reshape(TOKENS, FEATURE_DIM)
```

```python
import functools

import jax
import jax.numpy as jnp
from jax import lax
from jax.experimental import pallas as pl
from jax.experimental.pallas import tpu as pltpu
from jax.sharding import PartitionSpec as P

FEATURE_DIM = 1152
ROWS = 256
LOG2E = 1.4426950408889634
LN2 = 0.6931471805599453
NT = (((1,), (1,)), ((), ()))
TN = (((0,), (0,)), ((), ()))
AXES = ("dp", "hst")
F32 = jnp.float32
BF16 = jnp.bfloat16


def place_of(index):
    dp, hst = divmod(index, 8)
    return hst % 4, (hst // 4) * 2 + (dp // 2) % 2, dp // 4, dp % 2


def index_of(x, y, z, core):
    x, y, z = x % 4, y % 4, z % 8
    return (z * 4 + (y % 2) * 2 + core) * 8 + (y // 2) * 4 + x


def x_step(steps, x, y, z, core):
    return x + steps, y, z, core


def q_step(steps, x, y, z, core):
    if y % 2 == 0:
        z = z - 1 if core == 0 else z
    else:
        z = z if core == 0 else z + 1
    return x, y + steps, z, 1 - core


def core_step(x, y, z, core):
    return x, y, z, 1 - core


def moved(value, step):
    pairs = [(i, index_of(*step(*place_of(i)))) for i in range(256)]
    return lax.ppermute(value, AXES, pairs)


def ring_gather(own, step):
    half = ROWS // 2
    before = moved(own, functools.partial(step, 1))
    after = moved(own, functools.partial(step, -1))
    far_a = moved(before[:half], functools.partial(step, 1))
    far_b = moved(after[half:], functools.partial(step, -1))
    return before, after, far_a, far_b


def ring_scatter(own, before, after, far, step):
    half = ROWS // 2
    got_a = moved(far[:half], functools.partial(step, 1))
    got_b = moved(far[half:], functools.partial(step, -1))
    after = jnp.concatenate([summed(after[:half], got_a), after[half:]])
    before = jnp.concatenate([before[:half], summed(before[half:], got_b)])
    from_before = moved(after, functools.partial(step, 1))
    from_after = moved(before, functools.partial(step, -1))
    return summed(own, from_before, from_after)


def summed(*terms):
    total = terms[0].astype(F32)
    for term in terms[1:]:
        total = total + term.astype(F32)
    return total.astype(BF16)


def pair_terms(product, factors, positive):
    z = product * factors[0] + factors[1]
    if positive is not None:
        z = jnp.where(positive, -z, z)
    e = jnp.exp2(-jnp.abs(z))
    u = 1.0 + e
    log_u = jnp.where(e < 2.0**-8, LOG2E * e * (1.0 - 0.5 * e), jnp.log2(u))
    softplus = jnp.maximum(z, 0.0) + log_u
    scale = factors[2]
    coefficient = jnp.where(z >= 0.0, scale, scale * e) * pltpu.reciprocal(u, approx=True)
    if positive is not None:
        coefficient = jnp.where(positive, -coefficient, coefficient)
    return coefficient, softplus


def tile_kernel(factors_ref, slot_ref, *refs):
    n_in = 4 + 8
    ins, outs = refs[:n_in], refs[n_in:]
    grad_image, grad_text, loss, images, texts, coef, sems = outs
    spots = [(ins[0], images.at[pl.ds(0, 256)]), (ins[1], images.at[pl.ds(256, 256)]),
             (ins[2], images.at[pl.ds(512, 256)]), (ins[3], images.at[pl.ds(768, 128)]),
             (ins[4], images.at[pl.ds(896, 128)]), (ins[5], texts.at[pl.ds(0, 256)]),
             (ins[6], texts.at[pl.ds(256, 256)]), (ins[7], texts.at[pl.ds(512, 256)]),
             (ins[8], texts.at[pl.ds(768, 128)]), (ins[9], texts.at[pl.ds(896, 128)]),
             (ins[10], texts.at[pl.ds(1024, 256)]), (ins[11], texts.at[pl.ds(1280, 256)])]
    copies = [pltpu.make_async_copy(a, b, sems.at[n]) for n, (a, b) in enumerate(spots)]
    for copy in copies:
        copy.start()
    factors = [factors_ref[n] for n in range(3)]
    columns = lax.broadcasted_iota(jnp.int32, (ROWS, ROWS), 1)
    needed = [(5,), (6,), (7,), (8, 9), (10,), (11,)]
    for n in range(5):
        copies[n].wait()
    sums = [None] * 4
    for t in range(6):
        for n in needed[t]:
            copies[n].wait()
        text = texts[pl.ds(t * ROWS, ROWS), :]
        for i in range(4):
            image = images[pl.ds(i * ROWS, ROWS), :]
            product = lax.dot_general(image, text, NT, preferred_element_type=F32)
            positive = None
            if t in (0, 3):
                place = slot_ref[pl.ds(i * ROWS, ROWS), pl.ds(t // 3, 1)]
                positive = columns == place
            coefficient, softplus = pair_terms(product, factors, positive)
            coef[pl.ds(i * ROWS, ROWS), pl.ds(t * ROWS, ROWS)] = coefficient.astype(BF16)
            part = softplus[:, :128] + softplus[:, 128:]
            sums[i] = part if sums[i] is None else sums[i] + part
        grad_text[pl.ds(t * ROWS, ROWS), :] = lax.dot_general(
            coef[:, pl.ds(t * ROWS, ROWS)], images[...], TN, preferred_element_type=F32
        ).astype(BF16)
    for i in range(4):
        loss[pl.ds(i, 1), :] = jnp.sum(sums[i].T, axis=0, keepdims=True)
        grad_image[pl.ds(i * ROWS, ROWS), :] = jnp.dot(
            coef[pl.ds(i * ROWS, ROWS), :], texts[...], preferred_element_type=F32
        ).astype(BF16)


def tile(factors, slots, *blocks):
    any_spec = pl.BlockSpec(memory_space=pl.ANY)
    vmem = pl.BlockSpec(memory_space=pltpu.VMEM)
    return pl.pallas_call(
        tile_kernel,
        name="tile",
        out_shape=(
            jax.ShapeDtypeStruct((1024, FEATURE_DIM), BF16),
            jax.ShapeDtypeStruct((1536, FEATURE_DIM), BF16),
            jax.ShapeDtypeStruct((8, ROWS), F32),
        ),
        in_specs=[pl.BlockSpec(memory_space=pltpu.SMEM), vmem] + [any_spec] * len(blocks),
        out_specs=(vmem, vmem, vmem),
        scratch_shapes=[
            pltpu.VMEM((1024, FEATURE_DIM), BF16),
            pltpu.VMEM((1536, FEATURE_DIM), BF16),
            pltpu.VMEM((1024, 1536), BF16),
            pltpu.SemaphoreType.DMA((len(blocks),)),
        ],
        compiler_params=pltpu.CompilerParams(vmem_limit_bytes=48 << 20),
        cost_estimate=pl.CostEstimate(
            flops=6 * 1024 * 1536 * FEATURE_DIM, bytes_accessed=12 << 20, transcendentals=0
        ),
    )(factors, slots, *blocks)


def on_device(images, texts, slot, heat, offset):
    scale = heat[0] / FEATURE_DIM
    factors = jnp.stack([scale * LOG2E, offset[0] * LOG2E, scale])
    at = lax.axis_index("hst")
    x, high = at % 4, at // 4
    places = [high * 4 + (x + step) % 4 for step in (0, -1, 1, 2)]
    wanted = jnp.concatenate(
        [lax.dynamic_slice_in_dim(slot[0], place * ROWS, ROWS) for place in places]
    )
    slots = jnp.stack([wanted - at * ROWS, wanted - (at ^ 4) * ROWS], axis=1)

    image_ring = ring_gather(images, x_step)
    text_ring = ring_gather(texts, q_step)
    other_own = moved(texts, core_step)
    other_far = moved(jnp.concatenate(text_ring[2:]), core_step)
    grad_image, grad_text, loss = tile(
        factors, slots, images, *image_ring, texts, *text_ring, other_own, other_far
    )
    gi = [grad_image[n * ROWS : (n + 1) * ROWS] for n in range(4)]
    gt = [grad_text[n * ROWS : (n + 1) * ROWS] for n in range(6)]
    grad_image = ring_scatter(gi[0], gi[1], gi[2], gi[3], x_step)
    far = summed(gt[3], moved(gt[5], core_step))
    own = gt[0].astype(F32) + moved(gt[4], core_step).astype(F32)
    grad_text = ring_scatter(own, gt[1], gt[2], far, q_step)
    total = loss[0]
    for n, step in ((1, -1), (2, 1), (3, 2)):
        total = total + moved(loss[n], functools.partial(x_step, step))
    return total * (LN2 / 6144), grad_image, grad_text


def solution(mesh):
    in_specs = (P(AXES, None), P(AXES, None), P("dp", None), P(), P())
    out_specs = (P(AXES), P(AXES, None), P(AXES, None))
    return jax.shard_map(
        on_device, mesh=mesh, in_specs=in_specs, out_specs=out_specs, check_vma=False
    )
```

```python
import functools

import jax
import jax.numpy as jnp
from jax import lax
from jax.experimental import pallas as pl
from jax.experimental.pallas import tpu as pltpu
from jax.sharding import PartitionSpec as P

FEATURE_DIM = 1152
ROWS = 256
LOG2E = 1.4426950408889634
LN2 = 0.6931471805599453
HBM = pl.BlockSpec(memory_space=pltpu.HBM)
VMEM = pl.BlockSpec(memory_space=pltpu.VMEM)
SMEM = pl.BlockSpec(memory_space=pltpu.SMEM)
NT = (((1,), (1,)), ((), ()))
TN = (((0,), (0,)), ((), ()))
STEPS = {"i0": 0, "i1": -1, "i2": 1, "i3": 2}
IMAGES = list(STEPS)
TEXTS = ["t0", "t1", "t2", "t3", "c0", "c3"]
HOMES = {"t0": 0, "t3": 4}
AXES = ("dp", "hst")
F32 = jnp.float32
BF16 = jnp.bfloat16


def place_of(index):
    dp, hst = divmod(index, 8)
    return hst % 4, (hst // 4) * 2 + (dp // 2) % 2, dp // 4, dp % 2


def index_of(x, y, z, core):
    x, y, z = x % 4, y % 4, z % 8
    return (z * 4 + (y % 2) * 2 + core) * 8 + (y // 2) * 4 + x


def x_step(steps, x, y, z, core):
    return x + (steps if core == 0 else -steps), y, z, core


def q_step(steps, x, y, z, core):
    in_plane = y % 2 != core
    if not in_plane:
        z = z - 1 if core == 0 else z + 1
    return x, y + (steps if in_plane else -steps), z, 1 - core


def core_step(x, y, z, core):
    return x, y, z, 1 - core


def moved(value, step):
    pairs = [(i, index_of(*step(*place_of(i)))) for i in range(256)]
    return lax.ppermute(value, AXES, pairs)


def pair_terms(product, factors, positive):
    z = product * factors[0] + factors[1]
    if positive is not None:
        z = jnp.where(positive, -z, z)
    e = jnp.exp2(-jnp.abs(z))
    u = 1.0 + e
    log_u = jnp.where(e < 2.0**-8, LOG2E * e * (1.0 - 0.5 * e), jnp.log2(u))
    softplus = jnp.maximum(z, 0.0) + log_u
    scale = factors[2]
    coefficient = jnp.where(z >= 0.0, scale, scale * e) * pltpu.reciprocal(u, approx=True)
    if positive is not None:
        coefficient = jnp.where(positive, -coefficient, coefficient)
    return coefficient, softplus


def pairs_kernel(plan, at_ref, factors_ref, slot_ref, *refs):
    pairs, image_names, text_names, old_names, loss_names, kept, framed = plan
    refs = list(refs)

    def take(names):
        return {name: refs.pop(0) for name in names}

    images, texts = take(image_names), take(text_names)
    old, losses = take(old_names), take(loss_names)
    new = take(image_names + text_names)
    copies = take(kept)
    (loss_out, coef) = refs
    for name in kept:
        copies[name][...] = {**images, **texts}[name][...]
    factors = [factors_ref[n] for n in range(3)]
    at = at_ref[0]
    columns = lax.broadcasted_iota(jnp.int32, (ROWS, ROWS), 1)
    sums, wanted = {}, {}

    def block(names, name):
        return pl.ds(names.index(name) * ROWS, ROWS)

    def place_wanted(i):
        if i not in wanted:
            place = ((at & 4) + ((at + STEPS[i] * at_ref[1]) & 3)) * ROWS
            row = slot_ref[:, pl.ds(pl.multiple_of(place, ROWS), ROWS)]
            wanted[i] = jnp.broadcast_to(row, (128, ROWS)).T[:, :1]
        return wanted[i]

    def spot(i, t):
        return coef.at[block(image_names, i), block(text_names, t)]

    for i, t in pairs:
        product = lax.dot_general(
            images[i][...], texts[t][...], NT, preferred_element_type=F32
        )
        positive = None
        if t in HOMES:
            positive = columns == place_wanted(i) - (at ^ HOMES[t]) * ROWS
        coefficient, softplus = pair_terms(product, factors, positive)
        spot(i, t)[...] = coefficient.astype(BF16)
        part = softplus[:, :128] + softplus[:, 128:]
        sums[i] = part if i not in sums else sums[i] + part

    for t in text_names:
        mine = [i for i in image_names if (i, t) in pairs]
        total = lax.dot_general(
            jnp.concatenate([spot(i, t)[...] for i in mine]),
            jnp.concatenate([images[i][...] for i in mine]),
            TN,
            preferred_element_type=F32,
        )
        if t in old:
            total = total + old[t][...].astype(F32)
        if "more" in old:
            total = total + old["more"][...].astype(F32)
        new[t][...] = total.astype(BF16)
    for n, i in enumerate(IMAGES):
        row = pl.ds(n, 1)
        if i not in sums:
            value = sum((ref[row, :] for ref in losses.values()), jnp.zeros((1, ROWS), F32))
            loss_out[row, :] = value
            continue
        mine = [t for t in text_names if (i, t) in pairs]
        total = jnp.dot(
            jnp.concatenate([spot(i, t)[...] for t in mine], axis=1),
            jnp.concatenate([texts[t][...] for t in mine]),
            preferred_element_type=F32,
        )
        if i in old:
            total = total + old[i][...].astype(F32)
        new[i][pl.ds(0, ROWS), :] = total.astype(BF16)
        value = jnp.sum(sums[i].T, axis=0, keepdims=True)
        value = sum((ref[row, :] for ref in losses.values()), value)
        loss_out[row, :] = value
        if i in framed:
            at_row = lax.broadcasted_iota(jnp.int32, (16, ROWS), 0)
            large = value.astype(BF16).astype(F32)
            both = jnp.where(at_row == 0, large, jnp.where(at_row == 1, value - large, 0.0))
            new[i][pl.ds(ROWS, 16), :] = jnp.zeros((16, FEATURE_DIM), BF16)
            new[i][pl.ds(ROWS, 16), pl.ds(0, ROWS)] = both.astype(BF16)


def pair_call(name, common, values, pairs, old=None, losses=(), kept=(), framed=()):
    old = old or {}
    image_names = [i for i in IMAGES if any(i == p[0] for p in pairs)]
    text_names = [t for t in TEXTS if any(t == p[1] for p in pairs)]
    old_names = [n for n in [*image_names, *text_names, "more"] if n in old]
    plan = (pairs, image_names, text_names, old_names, list(range(len(losses))), kept, framed)
    blocks = [values[n] for n in image_names + text_names] + [old[n] for n in old_names]
    names = [*image_names, *text_names, *kept]
    rows = [ROWS + 16 if n in framed else ROWS for n in image_names] + [ROWS] * (
        len(text_names) + len(kept)
    )
    out = pl.pallas_call(
        functools.partial(pairs_kernel, plan),
        name=name,
        out_shape=[jax.ShapeDtypeStruct((r, FEATURE_DIM), BF16) for r in rows]
        + [jax.ShapeDtypeStruct((8, ROWS), F32)],
        in_specs=[SMEM, SMEM, VMEM] + [VMEM] * (len(blocks) + len(losses)),
        out_specs=[VMEM] * (len(rows) + 1),
        scratch_shapes=[pltpu.VMEM((len(image_names) * ROWS, len(text_names) * ROWS), BF16)],
        compiler_params=pltpu.CompilerParams(vmem_limit_bytes=24 << 20),
        cost_estimate=pl.CostEstimate(
            flops=6 * len(pairs) * ROWS * ROWS * FEATURE_DIM,
            bytes_accessed=2 * ROWS * FEATURE_DIM * (len(blocks) + len(rows)),
            transcendentals=0,
        ),
    )(*common, *blocks, *losses)
    grads = dict(zip(image_names + text_names, out))
    return {**old, **grads}, out[-1], list(out[len(image_names) + len(text_names) : -1])


def joined_kernel(left, right, out):
    rows = pl.ds(0, ROWS)
    out[rows, :] = (left[rows, :].astype(F32) + right[rows, :].astype(F32)).astype(BF16)
    if out.shape[0] > ROWS:
        rows = pl.ds(ROWS, 16)
        both = left[rows, :].astype(F32) + right[rows, :].astype(F32)
        value = both[0:1] + both[1:2]
        at_row = lax.broadcasted_iota(jnp.int32, both.shape, 0)
        large = value.astype(BF16).astype(F32)
        out[rows, :] = jnp.where(
            at_row == 0, large, jnp.where(at_row == 1, value - large, 0.0)
        ).astype(BF16)


def joined(left, right):
    return pl.pallas_call(
        joined_kernel,
        name="joined",
        out_shape=jax.ShapeDtypeStruct(left.shape, BF16),
        in_specs=[VMEM, VMEM],
        out_specs=VMEM,
        compiler_params=pltpu.CompilerParams(vmem_limit_bytes=16 << 20),
        cost_estimate=pl.CostEstimate(
            flops=ROWS * FEATURE_DIM, bytes_accessed=6 * ROWS * FEATURE_DIM, transcendentals=0
        ),
    )(left, right)


def summed(*terms):
    total = terms[0][:ROWS].astype(F32)
    for term in terms[1:]:
        total = total + term[:ROWS].astype(F32)
    return total.astype(BF16)


def tied(value, *others):
    return lax.optimization_barrier((value, *others))[0]


def on_device(images, texts, slot, heat, offset):
    scale = heat[0] / FEATURE_DIM
    factors = jnp.stack([scale * LOG2E, offset[0] * LOG2E, scale])
    way = 1 - 2 * (lax.axis_index("dp") & 1)
    at = jnp.stack([lax.axis_index("hst"), way]).astype(jnp.int32)
    call = functools.partial(pair_call, common=(at, factors, slot))

    def xs(value, n):
        with jax.named_scope("x"):
            return moved(value, functools.partial(x_step, n))

    def qs(value, n):
        with jax.named_scope("q"):
            return moved(value, functools.partial(q_step, n))

    def across(value):
        with jax.named_scope("core"):
            return moved(value, core_step)

    v = {"i0": images, "t0": texts}
    v["t1"], v["i1"] = qs(texts, 1), xs(images, 1)
    v["t2"], v["i2"] = qs(texts, -1), xs(images, -1)
    v["c0"] = across(texts)
    g, loss, (v["i0"], v["t0"]) = call(
        "own", values=v, pairs=[("i0", "t0"), ("i0", "c0")], kept=("i0", "t0")
    )
    v["t3"] = qs(tied(v["t1"], loss), 1)
    v["i3"] = xs(tied(v["i1"], loss), 1)
    g, loss, _ = call(
        "near", values=v, old=g, losses=(loss,),
        pairs=[("i1", "t1"), ("i1", "t2"), ("i2", "t1"), ("i2", "t2"), ("i0", "t1"),
               ("i0", "t2"), ("i1", "t0"), ("i1", "c0"), ("i2", "t0"), ("i2", "c0")],
    )
    v["c3"] = across(tied(v["t3"], loss))
    g, loss, _ = call(
        "third", values=v, old=g, losses=(loss,),
        pairs=[("i3", t) for t in ("t1", "t2", "t0", "c0")],
    )
    from_next = qs(g["t1"], -1)
    from_core = across(g["c0"])
    g, loss, _ = call(
        "across", values=v, old=g, losses=(loss,), pairs=[(i, "c3") for i in IMAGES]
    )
    far_core = across(g["c3"])
    g, loss, _ = call(
        "far", values=v, old=g, losses=(loss,), pairs=[("i3", "t3"), ("i1", "t3")],
        framed=("i1", "i3"),
    )
    image_far = xs(g["i3"], 1)
    image_next = xs(g["i1"], -1)
    g, loss, _ = call(
        "rest", values=v, old={**g, "more": far_core}, losses=(loss,),
        pairs=[("i0", "t3"), ("i2", "t3")], framed=("i2",),
    )
    text_far = qs(g["t3"], 1)
    text_prev = qs(joined(g["t2"], text_far), 1)
    image_prev = xs(joined(g["i2"], tied(image_far, text_far)), 1)
    row_loss = loss[0]
    for s in (image_next, image_prev):
        row_loss = row_loss + s[ROWS, :ROWS].astype(F32) + s[ROWS + 1, :ROWS].astype(F32)
    grad_image = summed(g["i0"], image_next, image_prev)
    grad_text = summed(g["t0"], from_core, from_next, text_prev)
    return row_loss * (LN2 / 6144), grad_image, grad_text


def solution(mesh):
    in_specs = (P(AXES, None), P(AXES, None), P("dp", None), P(), P())
    out_specs = (P(AXES), P(AXES, None), P(AXES, None))
    return jax.shard_map(
        on_device, mesh=mesh, in_specs=in_specs, out_specs=out_specs, check_vma=False
    )
```

```python
import functools

import jax
import jax.numpy as jnp
from jax import lax
from jax.experimental import pallas as pl
from jax.experimental.pallas import tpu as pltpu
from jax.sharding import PartitionSpec as P

FEATURE_DIM = 1152
ROWS = 256
LOG2E = 1.4426950408889634
LN2 = 0.6931471805599453
HBM = pl.BlockSpec(memory_space=pltpu.HBM)
VMEM = pl.BlockSpec(memory_space=pltpu.VMEM)
SMEM = pl.BlockSpec(memory_space=pltpu.SMEM)
NT = (((1,), (1,)), ((), ()))
TN = (((0,), (0,)), ((), ()))
STEPS = {"i0": 0, "i1": -1, "i2": 1, "i3": 2}
IMAGES = list(STEPS)
TEXTS = ["t0", "t1", "t2", "t3", "c0", "c3"]
HOMES = {"t0": 0, "t3": 4}
AXES = ("dp", "hst")
F32 = jnp.float32
BF16 = jnp.bfloat16


def place_of(index):
    dp, hst = divmod(index, 8)
    return hst % 4, (hst // 4) * 2 + (dp // 2) % 2, dp // 4, dp % 2


def index_of(x, y, z, core):
    x, y, z = x % 4, y % 4, z % 8
    return (z * 4 + (y % 2) * 2 + core) * 8 + (y // 2) * 4 + x


def x_step(steps, x, y, z, core):
    return x + (steps if core == 0 else -steps), y, z, core


def q_step(steps, x, y, z, core):
    in_plane = y % 2 != core
    if not in_plane:
        z = z - 1 if core == 0 else z + 1
    return x, y + (steps if in_plane else -steps), z, 1 - core


def core_step(x, y, z, core):
    return x, y, z, 1 - core


def moved(value, step):
    pairs = [(i, index_of(*step(*place_of(i)))) for i in range(256)]
    return lax.ppermute(value, AXES, pairs)


def pair_terms(product, factors, positive):
    z = product * factors[0] + factors[1]
    if positive is not None:
        z = jnp.where(positive, -z, z)
    e = jnp.exp2(-jnp.abs(z))
    u = 1.0 + e
    log_u = jnp.where(e < 2.0**-8, LOG2E * e * (1.0 - 0.5 * e), jnp.log2(u))
    softplus = jnp.maximum(z, 0.0) + log_u
    scale = factors[2]
    coefficient = jnp.where(z >= 0.0, scale, scale * e) * pltpu.reciprocal(u, approx=True)
    if positive is not None:
        coefficient = jnp.where(positive, -coefficient, coefficient)
    return coefficient, softplus


def pairs_kernel(plan, at_ref, factors_ref, slot_ref, *refs):
    pairs, names, old_names, known, n_loss, grads, fetched, framed = plan
    refs = list(refs)

    def take(keys):
        return {key: refs.pop(0) for key in keys}

    blocks, old = take(names), take(old_names)
    known_refs, loss_refs = take(range(len(known))), take(range(n_loss))
    new, copies = take(list(grads)), take(fetched)
    loss_out, coef = refs.pop(0), refs.pop(0)
    if fetched:
        sources = {**blocks, "slot": slot_ref}
        moves = [
            pltpu.make_async_copy(sources[name], copies[name], refs[0].at[n])
            for n, name in enumerate(fetched)
        ]
        for move in moves:
            move.start()
        for move in moves:
            move.wait()
        blocks = {**blocks, **copies}
        slot_ref = copies["slot"]
    images = [n for n in IMAGES if any(n == i for i, _ in pairs)]
    texts = [n for n in TEXTS if any(n == t for _, t in pairs)]
    factors = [factors_ref[n] for n in range(3)]
    at = at_ref[0]
    columns = lax.broadcasted_iota(jnp.int32, (ROWS, ROWS), 1)
    sums, wanted, spots = {}, {}, {}

    def placed(ref, rows, cols):
        for i in rows:
            for t in cols:
                at_row, at_col = rows.index(i) * ROWS, cols.index(t) * ROWS
                spots[i, t] = ref.at[pl.ds(at_row, ROWS), pl.ds(at_col, ROWS)]

    for n, (rows, cols) in enumerate(known):
        placed(known_refs[n], rows, cols)
    placed(coef, images, texts)

    def place_wanted(i):
        if i not in wanted:
            place = ((at & 4) + ((at + STEPS[i] * at_ref[1]) & 3)) * ROWS
            row = slot_ref[:, pl.ds(pl.multiple_of(place, ROWS), ROWS)]
            wanted[i] = jnp.broadcast_to(row, (128, ROWS)).T[:, :1]
        return wanted[i]

    for i, t in pairs:
        product = lax.dot_general(
            blocks[i][...], blocks[t][...], NT, preferred_element_type=F32
        )
        positive = None
        if t in HOMES:
            positive = columns == place_wanted(i) - (at ^ HOMES[t]) * ROWS
        coefficient, softplus = pair_terms(product, factors, positive)
        spots[i, t][...] = coefficient.astype(BF16)
        part = softplus[:, :128] + softplus[:, 128:]
        sums[i] = part if i not in sums else sums[i] + part

    values = {}
    for n, i in enumerate(IMAGES):
        row = pl.ds(n, 1)
        value = jnp.zeros((1, ROWS), F32)
        if i in sums:
            value = jnp.sum(sums[i].T, axis=0, keepdims=True)
        for ref in loss_refs.values():
            value = value + ref[row, :]
        loss_out[row, :] = values[i] = value

    for name, partners in grads.items():
        others = jnp.concatenate([blocks[p][...] for p in partners])
        if name in IMAGES:
            weights = jnp.concatenate([spots[name, p][...] for p in partners], axis=1)
            total = jnp.dot(weights, others, preferred_element_type=F32)
        else:
            weights = jnp.concatenate([spots[p, name][...] for p in partners])
            total = lax.dot_general(weights, others, TN, preferred_element_type=F32)
        if name in old:
            total = total + old[name][...].astype(F32)
        if name == "t3" and "more" in old:
            total = total + old["more"][...].astype(F32)
        new[name][pl.ds(0, ROWS), :] = total.astype(BF16)
        if name in framed:
            at_row = lax.broadcasted_iota(jnp.int32, (16, ROWS), 0)
            large = values[name].astype(BF16).astype(F32)
            small = values[name] - large
            both = jnp.where(at_row == 0, large, jnp.where(at_row == 1, small, 0.0))
            new[name][pl.ds(ROWS, 16), :] = jnp.zeros((16, FEATURE_DIM), BF16)
            new[name][pl.ds(ROWS, 16), pl.ds(0, ROWS)] = both.astype(BF16)


def pair_call(
    name, common, values, pairs, grads, old=None, known=(), losses=(), fetched=(), framed=()
):
    old = old or {}
    images = [n for n in IMAGES if any(n == i for i, _ in pairs)]
    texts = [n for n in TEXTS if any(n == t for _, t in pairs)]
    partners = [p for ps in grads.values() for p in ps]
    names = [n for n in [*IMAGES, *TEXTS] if n in images + texts + partners]
    old_names = [n for n in [*grads, "more"] if n in old]
    known_at = [(rows, cols) for rows, cols, _ in known]
    plan = (pairs, names, old_names, known_at, len(losses), grads, fetched, framed)
    block_specs = [HBM if n in fetched else VMEM for n in names]
    operands = [
        *(values[n] for n in names), *(old[n] for n in old_names),
        *(ref for _, _, ref in known), *losses,
    ]
    rows = [ROWS + 16 if n in framed else ROWS for n in grads]
    shapes = [jax.ShapeDtypeStruct((r, FEATURE_DIM), BF16) for r in rows]
    shapes += [
        jax.ShapeDtypeStruct(common[2].shape, jnp.int32)
        if n == "slot"
        else jax.ShapeDtypeStruct((ROWS, FEATURE_DIM), BF16)
        for n in fetched
    ]
    shapes += [
        jax.ShapeDtypeStruct((8, ROWS), F32),
        jax.ShapeDtypeStruct((max(len(images), 1) * ROWS, max(len(texts), 1) * ROWS), BF16),
    ]
    out = pl.pallas_call(
        functools.partial(pairs_kernel, plan),
        name=name,
        out_shape=shapes,
        in_specs=[SMEM, SMEM, HBM if fetched else VMEM, *block_specs]
        + [VMEM] * (len(operands) - len(names)),
        out_specs=[VMEM] * len(shapes),
        scratch_shapes=[pltpu.SemaphoreType.DMA((len(fetched),))] if fetched else [],
        compiler_params=pltpu.CompilerParams(vmem_limit_bytes=24 << 20),
        cost_estimate=pl.CostEstimate(
            flops=2 * (len(pairs) + len(partners)) * ROWS * ROWS * FEATURE_DIM,
            bytes_accessed=2 * ROWS * FEATURE_DIM * (len(operands) + len(shapes)),
            transcendentals=0,
        ),
    )(*common, *operands)
    new = dict(zip([*grads, *(f"{n} block" for n in fetched)], out))
    return {**old, **new}, out[-2], (images, texts, out[-1])


def joined_kernel(left, right, out):
    rows = pl.ds(0, ROWS)
    out[rows, :] = (left[rows, :].astype(F32) + right[rows, :].astype(F32)).astype(BF16)
    if out.shape[0] > ROWS:
        rows = pl.ds(ROWS, 16)
        both = left[rows, :].astype(F32) + right[rows, :].astype(F32)
        value = both[0:1] + both[1:2]
        at_row = lax.broadcasted_iota(jnp.int32, both.shape, 0)
        large = value.astype(BF16).astype(F32)
        out[rows, :] = jnp.where(
            at_row == 0, large, jnp.where(at_row == 1, value - large, 0.0)
        ).astype(BF16)


def joined(left, right):
    return pl.pallas_call(
        joined_kernel,
        name="joined",
        out_shape=jax.ShapeDtypeStruct(left.shape, BF16),
        in_specs=[VMEM, VMEM],
        out_specs=VMEM,
        compiler_params=pltpu.CompilerParams(vmem_limit_bytes=16 << 20),
        cost_estimate=pl.CostEstimate(
            flops=ROWS * FEATURE_DIM, bytes_accessed=6 * ROWS * FEATURE_DIM, transcendentals=0
        ),
    )(left, right)


def summed(*terms):
    total = terms[0][:ROWS].astype(F32)
    for term in terms[1:]:
        total = total + term[:ROWS].astype(F32)
    return total.astype(BF16)


def tied(value, *others):
    return lax.optimization_barrier((value, *others))[0]


def on_device(images, texts, slot, heat, offset):
    scale = heat[0] / FEATURE_DIM
    factors = jnp.stack([scale * LOG2E, offset[0] * LOG2E, scale])
    way = 1 - 2 * (lax.axis_index("dp") & 1)
    at = jnp.stack([lax.axis_index("hst"), way]).astype(jnp.int32)
    common = (at, factors, slot)

    def xs(value, n):
        with jax.named_scope("x"):
            return moved(value, functools.partial(x_step, n))

    def qs(value, n):
        with jax.named_scope("q"):
            return moved(value, functools.partial(q_step, n))

    def across(value):
        with jax.named_scope("core"):
            return moved(value, core_step)

    v = {"i0": images, "t0": texts}
    v["t1"], v["i1"] = qs(texts, 1), xs(images, 1)
    v["t2"], v["i2"] = qs(texts, -1), xs(images, -1)
    v["c0"] = across(texts)
    near = ("t1", "t2", "t0", "c0")
    g, loss, _ = pair_call(
        "own", common, v, [("i0", "t0"), ("i0", "c0")],
        {"i0": ("t0", "c0"), "t0": ("i0",), "c0": ("i0",)}, fetched=("i0", "t0", "slot"),
    )
    v = {**v, "i0": g["i0 block"], "t0": g["t0 block"]}
    call = functools.partial(pair_call, common=(at, factors, g["slot block"]))
    v["t3"] = qs(tied(v["t1"], loss), 1)
    v["i3"] = xs(tied(v["i1"], loss), 1)
    g, loss, _ = call(
        "near", values=v, old=g, losses=(loss,),
        pairs=[(i, t) for i in ("i1", "i2") for t in near] + [("i0", "t1"), ("i0", "t2")],
        grads={
            "i0": ("t1", "t2"), "i1": near, "i2": near, "t0": ("i1", "i2"),
            "c0": ("i1", "i2"), "t1": ("i0", "i1", "i2"), "t2": ("i0", "i1", "i2"),
        },
    )
    v["c3"] = across(tied(v["t3"], loss))
    g, loss, from_third = call(
        "third", values=v, old=g, losses=(loss,), pairs=[("i3", t) for t in near],
        grads={"t1": ("i3",), "i3": near},
    )
    g, loss, from_across = call(
        "across", values=v, old=g, losses=(loss,), pairs=[(i, "c3") for i in IMAGES],
        grads={"c3": IMAGES},
    )
    far_core = across(g["c3"])
    g, loss, from_far = call(
        "far", values=v, old=g, losses=(loss,), pairs=[("i3", "t3"), ("i1", "t3")],
        known=(from_across,), grads={"i3": ("c3", "t3"), "i1": ("c3", "t3")},
        framed=("i1", "i3"),
    )
    image_far = xs(g["i3"], 1)
    image_next = xs(g["i1"], -1)
    g, loss, from_rest = call(
        "rest", values=v, old={**g, "more": far_core}, losses=(loss,),
        pairs=[("i0", "t3"), ("i2", "t3")], known=(from_far,), grads={"t3": IMAGES},
    )
    text_far = qs(g["t3"], 1)
    g, _, _ = call(
        "wrap", values=v, old=g, losses=(loss,), pairs=[],
        known=(from_third, from_across, from_rest),
        grads={
            "t2": ("i3",), "c0": ("i3",), "t0": ("i3",), "i2": ("c3", "t3"), "i0": ("c3", "t3")
        },
        framed=("i2",),
    )
    from_core = across(g["c0"])
    from_next = qs(tied(g["t1"], g["c0"]), -1)
    text_prev = qs(joined(g["t2"], text_far), 1)
    image_prev = xs(joined(g["i2"], tied(image_far, text_far, image_next)), 1)
    row_loss = loss[0]
    for s in (image_next, image_prev):
        row_loss = row_loss + s[ROWS, :ROWS].astype(F32) + s[ROWS + 1, :ROWS].astype(F32)
    grad_image = summed(g["i0"], image_next, image_prev)
    grad_text = summed(g["t0"], from_core, from_next, text_prev)
    return row_loss * (LN2 / 6144), grad_image, grad_text


def solution(mesh):
    in_specs = (P(AXES, None), P(AXES, None), P("dp", None), P(), P())
    out_specs = (P(AXES), P(AXES, None), P(AXES, None))
    return jax.shard_map(
        on_device, mesh=mesh, in_specs=in_specs, out_specs=out_specs, check_vma=False
    )
```

```python
import functools

import jax
import jax.numpy as jnp
from jax import lax
from jax.experimental import pallas as pl
from jax.experimental.pallas import tpu as pltpu
from jax.sharding import PartitionSpec as P

FEATURE_DIM = 1152
ROWS = 256
LOG2E = 1.4426950408889634
LN2 = 0.6931471805599453
HBM = pl.BlockSpec(memory_space=pltpu.HBM)
VMEM = pl.BlockSpec(memory_space=pltpu.VMEM)
SMEM = pl.BlockSpec(memory_space=pltpu.SMEM)
NT = (((1,), (1,)), ((), ()))
TN = (((0,), (0,)), ((), ()))
STEPS = {"i0": 0, "i1": -1, "i2": 1, "i3": 2}
IMAGES = list(STEPS)
TEXTS = ["t0", "t1", "t2", "t3", "c0", "c3"]
HOMES = {"t0": 0, "t3": 4}
AXES = ("dp", "hst")
F32 = jnp.float32
BF16 = jnp.bfloat16


def place_of(index):
    dp, hst = divmod(index, 8)
    return hst % 4, (hst // 4) * 2 + (dp // 2) % 2, dp // 4, dp % 2


def index_of(x, y, z, core):
    x, y, z = x % 4, y % 4, z % 8
    return (z * 4 + (y % 2) * 2 + core) * 8 + (y // 2) * 4 + x


def x_step(steps, x, y, z, core):
    return x + (steps if core == 0 else -steps), y, z, core


def q_step(steps, x, y, z, core):
    in_plane = y % 2 != core
    if not in_plane:
        z = z - 1 if core == 0 else z + 1
    return x, y + (steps if in_plane else -steps), z, 1 - core


def core_step(x, y, z, core):
    return x, y, z, 1 - core


def moved(value, step):
    pairs = [(i, index_of(*step(*place_of(i)))) for i in range(256)]
    return lax.ppermute(value, AXES, pairs)


def pair_terms(product, factors, positive):
    z = product * factors[0] + factors[1]
    if positive is not None:
        z = jnp.where(positive, -z, z)
    e = jnp.exp2(-jnp.abs(z))
    u = 1.0 + e
    log_u = jnp.where(e < 2.0**-8, LOG2E * e * (1.0 - 0.5 * e), jnp.log2(u))
    softplus = jnp.maximum(z, 0.0) + log_u
    scale = factors[2]
    coefficient = jnp.where(z >= 0.0, scale, scale * e) * pltpu.reciprocal(u, approx=True)
    if positive is not None:
        coefficient = jnp.where(positive, -coefficient, coefficient)
    return coefficient, softplus


def pairs_kernel(plan, at_ref, factors_ref, slot_ref, *refs):
    pairs, names, old_names, known, n_loss, grads, fetched, framed = plan
    refs = list(refs)

    def take(keys):
        return {key: refs.pop(0) for key in keys}

    blocks, old = take(names), take(old_names)
    known_refs, loss_refs = take(range(len(known))), take(range(n_loss))
    new, copies = take(list(grads)), take(fetched)
    loss_out, coef = refs.pop(0), refs.pop(0)
    if fetched:
        sources = {**blocks, "slot": slot_ref}
        moves = [
            pltpu.make_async_copy(sources[name], copies[name], refs[0].at[n])
            for n, name in enumerate(fetched)
        ]
        for move in moves:
            move.start()
        for move in moves:
            move.wait()
        blocks = {**blocks, **copies}
        slot_ref = copies["slot"]
    images = [n for n in IMAGES if any(n == i for i, _ in pairs)]
    texts = [n for n in TEXTS if any(n == t for _, t in pairs)]
    factors = [factors_ref[n] for n in range(3)]
    at = at_ref[0]
    columns = lax.broadcasted_iota(jnp.int32, (ROWS, ROWS), 1)
    sums, wanted, spots = {}, {}, {}

    def placed(ref, rows, cols):
        for i in rows:
            for t in cols:
                at_row, at_col = rows.index(i) * ROWS, cols.index(t) * ROWS
                spots[i, t] = ref.at[pl.ds(at_row, ROWS), pl.ds(at_col, ROWS)]

    for n, (rows, cols) in enumerate(known):
        placed(known_refs[n], rows, cols)
    placed(coef, images, texts)

    def place_wanted(i):
        if i not in wanted:
            place = ((at & 4) + ((at + STEPS[i] * at_ref[1]) & 3)) * ROWS
            row = slot_ref[:, pl.ds(pl.multiple_of(place, ROWS), ROWS)]
            wanted[i] = jnp.broadcast_to(row, (128, ROWS)).T[:, :1]
        return wanted[i]

    for i, t in pairs:
        product = lax.dot_general(
            blocks[i][...], blocks[t][...], NT, preferred_element_type=F32
        )
        positive = None
        if t in HOMES:
            positive = columns == place_wanted(i) - (at ^ HOMES[t]) * ROWS
        coefficient, softplus = pair_terms(product, factors, positive)
        spots[i, t][...] = coefficient.astype(BF16)
        part = softplus[:, :128] + softplus[:, 128:]
        sums[i] = part if i not in sums else sums[i] + part

    values = {}
    for n, i in enumerate(IMAGES):
        row = pl.ds(n, 1)
        value = jnp.zeros((1, ROWS), F32)
        if i in sums:
            value = jnp.sum(sums[i].T, axis=0, keepdims=True)
        for ref in loss_refs.values():
            value = value + ref[row, :]
        loss_out[row, :] = values[i] = value

    for name, partners in grads.items():
        others = jnp.concatenate([blocks[p][...] for p in partners])
        if name in IMAGES:
            weights = jnp.concatenate([spots[name, p][...] for p in partners], axis=1)
            total = jnp.dot(weights, others, preferred_element_type=F32)
        else:
            weights = jnp.concatenate([spots[p, name][...] for p in partners])
            total = lax.dot_general(weights, others, TN, preferred_element_type=F32)
        if name in old:
            total = total + old[name][...].astype(F32)
        if name == "t3" and "more" in old:
            total = total + old["more"][...].astype(F32)
        new[name][pl.ds(0, ROWS), :] = total.astype(BF16)
        if name in framed:
            at_row = lax.broadcasted_iota(jnp.int32, (16, ROWS), 0)
            large = values[name].astype(BF16).astype(F32)
            small = values[name] - large
            both = jnp.where(at_row == 0, large, jnp.where(at_row == 1, small, 0.0))
            new[name][pl.ds(ROWS, 16), :] = jnp.zeros((16, FEATURE_DIM), BF16)
            new[name][pl.ds(ROWS, 16), pl.ds(0, ROWS)] = both.astype(BF16)


def pair_call(
    name, common, values, pairs, grads, old=None, known=(), losses=(), fetched=(), framed=()
):
    old = old or {}
    images = [n for n in IMAGES if any(n == i for i, _ in pairs)]
    texts = [n for n in TEXTS if any(n == t for _, t in pairs)]
    partners = [p for ps in grads.values() for p in ps]
    names = [n for n in [*IMAGES, *TEXTS] if n in images + texts + partners]
    old_names = [n for n in [*grads, "more"] if n in old]
    known_at = [(rows, cols) for rows, cols, _ in known]
    plan = (pairs, names, old_names, known_at, len(losses), grads, fetched, framed)
    block_specs = [HBM if n in fetched else VMEM for n in names]
    operands = [
        *(values[n] for n in names), *(old[n] for n in old_names),
        *(ref for _, _, ref in known), *losses,
    ]
    rows = [ROWS + 16 if n in framed else ROWS for n in grads]
    shapes = [jax.ShapeDtypeStruct((r, FEATURE_DIM), BF16) for r in rows]
    shapes += [
        jax.ShapeDtypeStruct(common[2].shape, jnp.int32)
        if n == "slot"
        else jax.ShapeDtypeStruct((ROWS, FEATURE_DIM), BF16)
        for n in fetched
    ]
    shapes += [
        jax.ShapeDtypeStruct((8, ROWS), F32),
        jax.ShapeDtypeStruct((max(len(images), 1) * ROWS, max(len(texts), 1) * ROWS), BF16),
    ]
    out = pl.pallas_call(
        functools.partial(pairs_kernel, plan),
        name=name,
        out_shape=shapes,
        in_specs=[SMEM, SMEM, HBM if fetched else VMEM, *block_specs]
        + [VMEM] * (len(operands) - len(names)),
        out_specs=[VMEM] * len(shapes),
        scratch_shapes=[pltpu.SemaphoreType.DMA((len(fetched),))] if fetched else [],
        compiler_params=pltpu.CompilerParams(vmem_limit_bytes=24 << 20),
        cost_estimate=pl.CostEstimate(
            flops=2 * (len(pairs) + len(partners)) * ROWS * ROWS * FEATURE_DIM,
            bytes_accessed=2 * ROWS * FEATURE_DIM * (len(operands) + len(shapes)),
            transcendentals=0,
        ),
    )(*common, *operands)
    new = dict(zip([*grads, *(f"{n} block" for n in fetched)], out))
    return {**old, **new}, out[-2], (images, texts, out[-1])


def joined_kernel(left, right, out):
    rows = pl.ds(0, ROWS)
    out[rows, :] = (left[rows, :].astype(F32) + right[rows, :].astype(F32)).astype(BF16)
    if out.shape[0] > ROWS:
        rows = pl.ds(ROWS, 16)
        both = left[rows, :].astype(F32) + right[rows, :].astype(F32)
        value = both[0:1] + both[1:2]
        at_row = lax.broadcasted_iota(jnp.int32, both.shape, 0)
        large = value.astype(BF16).astype(F32)
        out[rows, :] = jnp.where(
            at_row == 0, large, jnp.where(at_row == 1, value - large, 0.0)
        ).astype(BF16)


def joined(left, right):
    return pl.pallas_call(
        joined_kernel,
        name="joined",
        out_shape=jax.ShapeDtypeStruct(left.shape, BF16),
        in_specs=[VMEM, VMEM],
        out_specs=VMEM,
        compiler_params=pltpu.CompilerParams(vmem_limit_bytes=16 << 20),
        cost_estimate=pl.CostEstimate(
            flops=ROWS * FEATURE_DIM, bytes_accessed=6 * ROWS * FEATURE_DIM, transcendentals=0
        ),
    )(left, right)


def summed(*terms):
    total = terms[0][:ROWS].astype(F32)
    for term in terms[1:]:
        total = total + term[:ROWS].astype(F32)
    return total.astype(BF16)


def tied(value, *others):
    return lax.optimization_barrier((value, *others))[0]


def on_device(images, texts, slot, heat, offset):
    scale = heat[0] / FEATURE_DIM
    factors = jnp.stack([scale * LOG2E, offset[0] * LOG2E, scale])
    way = 1 - 2 * (lax.axis_index("dp") & 1)
    at = jnp.stack([lax.axis_index("hst"), way]).astype(jnp.int32)
    common = (at, factors, slot)

    def xs(value, n):
        with jax.named_scope("x"):
            return moved(value, functools.partial(x_step, n))

    def qs(value, n):
        with jax.named_scope("q"):
            return moved(value, functools.partial(q_step, n))

    def across(value):
        with jax.named_scope("core"):
            return moved(value, core_step)

    v = {"i0": images, "t0": texts}
    v["t1"], v["i1"] = qs(texts, 1), xs(images, 1)
    v["t2"], v["i2"] = qs(texts, -1), xs(images, -1)
    v["c0"] = across(texts)
    near = ("t1", "t2", "t0", "c0")
    g, loss, _ = pair_call(
        "own", common, v, [("i0", "t0"), ("i0", "c0")],
        {"i0": ("t0", "c0"), "t0": ("i0",), "c0": ("i0",)}, fetched=("i0", "t0", "slot"),
    )
    v = {**v, "i0": g["i0 block"], "t0": g["t0 block"]}
    call = functools.partial(pair_call, common=(at, factors, g["slot block"]))
    v["t3"] = qs(tied(v["t1"], loss), 1)
    v["i3"] = xs(tied(v["i1"], loss), 1)
    g, loss, _ = call(
        "near", values=v, old=g, losses=(loss,),
        pairs=[(i, t) for i in ("i1", "i2") for t in near] + [("i0", "t1"), ("i0", "t2")],
        grads={
            "i0": ("t1", "t2"), "i1": near, "i2": near, "t0": ("i1", "i2"),
            "c0": ("i1", "i2"), "t1": ("i0", "i1", "i2"), "t2": ("i0", "i1", "i2"),
        },
    )
    v["c3"] = across(tied(v["t3"], loss))
    g, loss, from_third = call(
        "third", values=v, old=g, losses=(loss,), pairs=[("i3", t) for t in near],
        grads={"t1": ("i3",), "i3": near},
    )
    g, loss, from_across = call(
        "across", values=v, old=g, losses=(loss,), pairs=[(i, "c3") for i in IMAGES],
        grads={"c3": IMAGES},
    )
    far_core = across(g["c3"])
    g, loss, from_far = call(
        "far", values=v, old=g, losses=(loss,), pairs=[("i3", "t3"), ("i1", "t3")],
        known=(from_across,), grads={"i3": ("c3", "t3"), "i1": ("c3", "t3")},
        framed=("i1", "i3"),
    )
    image_far = xs(g["i3"], 1)
    image_next = xs(g["i1"], -1)
    g, loss, from_rest = call(
        "rest", values=v, old={**g, "more": far_core}, losses=(loss,),
        pairs=[("i0", "t3"), ("i2", "t3")], known=(from_far,), grads={"t3": IMAGES},
    )
    text_far = qs(g["t3"], 1)
    g, _, _ = call(
        "wrap", values=v, old=g, losses=(loss,), pairs=[],
        known=(from_third, from_across, from_rest),
        grads={
            "t2": ("i3",), "c0": ("i3",), "t0": ("i3",), "i2": ("c3", "t3"), "i0": ("c3", "t3")
        },
        framed=("i2",),
    )
    from_core = across(g["c0"])
    from_next = qs(tied(g["t1"], g["c0"]), -1)
    text_prev = qs(joined(g["t2"], tied(text_far, image_far)), 1)
    image_prev = xs(joined(g["i2"], tied(image_far, text_far, image_next)), 1)
    row_loss = loss[0]
    for s in (image_next, image_prev):
        row_loss = row_loss + s[ROWS, :ROWS].astype(F32) + s[ROWS + 1, :ROWS].astype(F32)
    grad_image = summed(g["i0"], image_next, image_prev)
    grad_text = summed(g["t0"], from_core, from_next, text_prev)
    return row_loss * (LN2 / 6144), grad_image, grad_text


def solution(mesh):
    in_specs = (P(AXES, None), P(AXES, None), P("dp", None), P(), P())
    out_specs = (P(AXES), P(AXES, None), P(AXES, None))
    return jax.shard_map(
        on_device, mesh=mesh, in_specs=in_specs, out_specs=out_specs, check_vma=False
    )
```
